256 devices in a mesh: dp: 4 (over x), expert: 64 (over z, y, core).
Axes of the slice: x: 4, y: 4, z: 8, core: 2. Of those that a mesh axis runs over, the one named last changes fastest.
Arguments:
- tokens: bfloat16 [32768, 2048], P(('dp', 'expert')), may hold values from -6 to 6
- out_grad: bfloat16 [32768, 2048], P(('dp', 'expert')), may hold values from -6 to 6
- routes: int32 [32768, 3], P(('dp', 'expert')), may hold values from 0 to 63, all different within a row; in each aligned block of 128 rows (0 to 127, 128 to 255, ...) at most 9 rows name the same one
- levels: int32 [32768, 3], P(('dp', 'expert')), may hold values from 16 to 255
- w_gate: bfloat16 [64, 2048, 768], P('expert', 'dp'), may hold values from -0.125 to 0.125
- w_up: bfloat16 [64, 2048, 768], P('expert', 'dp'), may hold values from -0.125 to 0.125
- w_down: bfloat16 [64, 768, 2048], P('expert', None, 'dp'), may hold values from -0.21875 to 0.21875
Outputs:
- grad_tokens: bfloat16 [32768, 2048], P(('dp', 'expert'))
- grad_gate_w: bfloat16 [64, 2048, 768], P('expert', 'dp')
- grad_up_w: bfloat16 [64, 2048, 768], P('expert', 'dp')
- grad_down_w: bfloat16 [64, 768, 2048], P('expert', None, 'dp')
The draws below stay inside these ranges and needn't reach their ends.
Inputs may be any that keep to these rules, and one draw needn't show every extreme that they name: `routes`: each row names 3 different experts. Among the 128 rows of one device no expert is named by more than 9 rows, a bound that some block reaches.
All inputs are finite; a program needn't handle non-finite values.
Results may differ from the reference program's by a relative error of at most 0.0065.
Values may be sent and summed in bfloat16 or wider, within the bound.
No kernel may reach another device: no remote copies, remote signals or barrier semaphores. Data moves between devices by JAX's collectives and lax.ppermute only.
A program may use at most 128 MiB of HBM per device.

```python
import math
import jax
import jax.numpy as jnp
import numpy as np
from jax import lax

D = 2048
FF = 768
TOP = 3
TOK_DEV = 128
EXPERTS = 64
CAP = 9
TOKENS = 32768


def plant(entries, key, smallest, largest):
    index_at = [jax.random.randint(jax.random.fold_in(key, axis), (), 0, length) for axis, length in enumerate(entries.shape)]
    longest = entries.shape.index(max(entries.shape))
    beside = index_at[:longest] + [(index_at[longest] + 1) % entries.shape[longest]] + index_at[longest + 1:]
    return entries.at[tuple(index_at)].set(smallest).at[tuple(beside)].set(largest)


def block_levels(rng, extent, shards, least, high):
    level = 1.0
    for position, blocks in shards:
        steps = jax.random.uniform(jax.random.fold_in(jax.random.fold_in(rng, 6), position), (blocks,), jnp.float32, least / len(shards), high / len(shards))
        level = level * jnp.repeat(jnp.exp(steps), extent[position] // blocks).reshape((-1,) + (1,) * (len(extent) - 1 - position))
    return level


def assign_block(rng, own, number, rows, amount, top, most, lean):
    sequence = jax.random.permutation(rng, amount)
    heavy_load, usual = portions_of(amount, rows * top, most, lean, True), portions_of(amount, rows * top, most, lean, False)
    places = jnp.arange(amount)

    def named(lengths, turn):
        used = int((lengths > 0).sum())
        fixed = max(1, used // 4)
        passed = fixed + (places - fixed + turn * (used - fixed)) % max(1, amount - fixed)
        return jnp.zeros((amount,), jnp.int32).at[sequence[jnp.where(places < fixed, places, passed)]].set(jnp.asarray(lengths, jnp.int32))

    lengths = jnp.where(number % 4 == 0, named(heavy_load, number // 4), named(usual, number - number // 4 - 1))
    mixed = jax.random.permutation(jax.random.fold_in(own, 3), amount)
    source_of, taker = mixed[0:amount // 2 * 2:2], mixed[1:amount // 2 * 2:2]
    slack = jnp.minimum(lengths[source_of] - 1, most - lengths[taker]) // 2
    slack = jnp.where((source_of == sequence[0]) | (taker == sequence[0]) | (lengths[taker] == 0), 0, jnp.maximum(slack, 0))
    passed = jax.random.randint(jax.random.fold_in(own, 4), (amount // 2,), 0, 1 << 20) % (slack + 1)
    lengths = lengths.at[source_of].add(-passed).at[taker].add(passed)
    items = jnp.searchsorted(jnp.cumsum(lengths), jnp.arange(rows * top), side="right").astype(jnp.int32)
    table = items.reshape(top, rows).T
    table = table[jax.random.permutation(jax.random.fold_in(own, 1), rows)]
    turn = jax.random.randint(jax.random.fold_in(own, 2), (rows, 1), 0, top)
    return jnp.take_along_axis(table, (jnp.arange(top)[None, :] + turn) % top, axis=1)


def portions_of(count, total, most, skew, full):
    weights = [(1 << 20) // math.isqrt(grade ** skew) + 1 for grade in range(1, count + 1)]
    largest = most if full else min(most, max(-(-total // count), total * weights[0] // sum(weights)))
    least = 1 if total - largest >= count - 1 else 0
    given, rest = [largest] + [least] * (count - 1), total - largest - least * (count - 1)
    while rest > 0:
        free = [i for i in range(1, count) if given[i] < largest] or [i for i in range(1, count) if given[i] < most]
        mass, left = sum([weights[i] for i in free]), rest
        for i in free:
            addition = min(most - given[i], max(1, left * weights[i] // mass), rest)
            given[i] = given[i] + addition
            rest = rest - addition
    return np.array(given)


def bell_draw(own_key, dims, spread, most, split=(), held_as=jnp.bfloat16):
    values = spread * jax.random.normal(own_key, dims, jnp.float32)
    if split:
        values = values * block_levels(own_key, dims, split, -0.22, 0.18)
    return jnp.clip(values, -most, most).astype(held_as)


def setup_inputs(seed: int = 0) -> dict:
    splits = jax.random.split(jax.random.key(seed), 8)
    tokens = bell_draw(splits[0], (TOKENS, D), 1.0, 6.0, ((0, 256),))
    out_grad = bell_draw(splits[1], (TOKENS, D), 1.0, 6.0, ((0, 256),))
    routes_keys = jax.random.split(jax.random.fold_in(splits[2], 1), TOKENS // TOK_DEV)
    routes_turns = jax.random.permutation(jax.random.fold_in(splits[2], 3), TOKENS // TOK_DEV)
    routes = jax.vmap(lambda own, number: assign_block(jax.random.fold_in(splits[2], 2), own, number, TOK_DEV, EXPERTS, TOP, CAP, 2))(routes_keys, routes_turns).reshape((TOKENS, TOP))
    levels = plant(jax.random.randint(splits[3], (TOKENS, TOP), 16, 256), jax.random.fold_in(splits[3], 1), 16, 255).astype(jnp.int32)
    w_gate = bell_draw(splits[4], (EXPERTS, D, FF), D ** -0.5, 0.125, ((0, 64), (1, 4)))
    w_up = bell_draw(splits[5], (EXPERTS, D, FF), D ** -0.5, 0.125, ((0, 64), (1, 4)))
    w_down = bell_draw(splits[6], (EXPERTS, FF, D), FF ** -0.5, 0.21875, ((0, 64), (2, 4)))
    return {"tokens": tokens, "out_grad": out_grad, "routes": routes, "levels": levels, "w_gate": w_gate, "w_up": w_up, "w_down": w_down}


def reference(tokens, out_grad, routes, levels, w_gate, w_up, w_down):
    pairs = TOKENS * TOP
    most_rows = CAP * (TOKENS // TOK_DEV)
    flat_expert = routes.reshape(-1).astype(jnp.int32)
    order = jnp.argsort(flat_expert, stable=True).astype(jnp.int32)
    counts = jnp.sum((flat_expert[:, None] == jnp.arange(EXPERTS, dtype=jnp.int32)[None, :]).astype(jnp.int32), axis=0)
    starts = (jnp.cumsum(counts) - counts).astype(jnp.int32)
    gains = levels.reshape(-1).astype(jnp.float32) / 256.0
    contract_rows = (((0,), (0,)), ((), ()))
    contract_cols = (((1,), (1,)), ((), ()))

    def one_expert(carry, expert):
        local = jnp.arange(most_rows, dtype=jnp.int32)
        valid = local < counts[expert]
        index = jnp.minimum(starts[expert] + local, pairs - 1).astype(jnp.int32)
        pair = jnp.where(valid, order[index], 0).astype(jnp.int32)
        token = (pair // TOP).astype(jnp.int32)
        keep = valid[:, None]
        rows = jnp.where(keep, tokens[token], jnp.zeros((), tokens.dtype))
        zgrad = jnp.where(keep, gains[pair][:, None] * out_grad[token].astype(jnp.float32), 0.0).astype(jnp.bfloat16)
        mat_gate = w_gate[expert]
        mat_up = w_up[expert]
        mat_down = w_down[expert]
        pre_gate = jnp.dot(rows, mat_gate, preferred_element_type=jnp.float32)
        pre_up = jnp.dot(rows, mat_up, preferred_element_type=jnp.float32)
        sigma = jax.nn.sigmoid(pre_gate)
        swish = pre_gate * sigma
        hidden = (swish * pre_up).astype(jnp.bfloat16)
        grad_hidden = lax.dot_general(zgrad, mat_down, contract_cols, preferred_element_type=jnp.float32)
        grad_gate = (grad_hidden * pre_up * sigma * (1.0 + pre_gate * (1.0 - sigma))).astype(jnp.bfloat16)
        grad_up = (grad_hidden * swish).astype(jnp.bfloat16)
        back = lax.dot_general(grad_gate, mat_gate, contract_cols, preferred_element_type=jnp.float32)
        back = back + lax.dot_general(grad_up, mat_up, contract_cols, preferred_element_type=jnp.float32)
        back = back.astype(jnp.bfloat16)
        gw_gate = lax.dot_general(rows, grad_gate, contract_rows, preferred_element_type=jnp.float32).astype(jnp.bfloat16)
        gw_up = lax.dot_general(rows, grad_up, contract_rows, preferred_element_type=jnp.float32).astype(jnp.bfloat16)
        gw_down = lax.dot_general(hidden, zgrad, contract_rows, preferred_element_type=jnp.float32).astype(jnp.bfloat16)
        target = jnp.where(valid, pair, pairs).astype(jnp.int32)
        carry = carry.at[target].set(back, mode="drop")
        return carry, (gw_gate, gw_up, gw_down)

    start_terms = jnp.zeros((pairs, D), jnp.bfloat16)
    terms, grads = lax.scan(one_expert, start_terms, jnp.arange(EXPERTS, dtype=jnp.int32))
    terms = terms.reshape(TOKENS, TOP, D)
    total = jnp.zeros((TOKENS, D), jnp.float32)
    for choice_k in range(TOP):
        total = total + terms[:, choice_k, :].astype(jnp.float32)
    return total.astype(jnp.bfloat16), grads[0], grads[1], grads[2]
```

```python
import jax
import jax.numpy as jnp
from jax import lax
from jax.sharding import Mesh, PartitionSpec as P

CAP = 9
ROWS0 = (((0,), (0,)), ((), ()))
COLS1 = (((1,), (1,)), ((), ()))
f32 = jnp.float32
bf16 = jnp.bfloat16


def shift(v, axis, step):
    n = lax.axis_size(axis)
    return lax.ppermute(v, axis, [(i, (i + step) % n) for i in range(n)])


def dot(a, b, dims=(((1,), (0,)), ((), ()))):
    return lax.dot_general(a, b, dims, preferred_element_type=f32)


def roll_cols(v, start):
    return lax.dynamic_slice(jnp.concatenate([v, v], axis=1), (0, start), v.shape)


def gather_x(w):
    half = w.shape[0] // 2
    right = shift(w, "x", -1)
    left = shift(w, "x", 1)
    far_a = shift(right[:half], "x", -1)
    far_b = shift(left[half:], "x", 1)
    return w, right, jnp.concatenate([far_a, far_b], axis=0), left


def scatter_x(term):
    far = term(2).astype(bf16)
    half = far.shape[0] // 2
    via_right = shift(far[:half], "x", 1)
    via_left = shift(far[half:], "x", -1)
    one, three = term(1), term(3)
    to_right = jnp.concatenate([one[:half] + via_right.astype(f32), one[half:]], axis=0)
    to_left = jnp.concatenate([three[:half], three[half:] + via_left.astype(f32)], axis=0)
    from_left = shift(to_right.astype(bf16), "x", 1)
    from_right = shift(to_left.astype(bf16), "x", -1)
    return (term(0) + from_left.astype(f32) + from_right.astype(f32)).astype(bf16)[None]


def per_device(tokens, out_grad, routes, levels, w_gate, w_up, w_down):
    tok, width = tokens.shape
    top = routes.shape[1]
    n_z, n_w, n_x = lax.axis_size("z"), lax.axis_size("w"), lax.axis_size("x")
    n_expert = n_z * n_w
    quarter = width // n_x
    me_x, me_z = lax.axis_index("x"), lax.axis_index("z")
    group = n_z * CAP
    slots = n_w * group

    named = [(routes[:, k : k + 1] == jnp.arange(n_expert)[None, :]).astype(f32) for k in range(top)]
    lower = (jnp.arange(tok)[:, None] > jnp.arange(tok)[None, :]).astype(bf16)
    before = dot(lower, sum(named).astype(bf16))
    rank = [jnp.sum(before * m, axis=1).astype(jnp.int32) for m in named]
    info = jnp.stack(
        [routes[:, k] * CAP + rank[k] for k in range(top)]
        + [levels[:, k] for k in range(top)]
        + [jnp.zeros((tok,), jnp.int32)] * (8 - 2 * top),
        axis=0,
    )
    info = lax.all_to_all(
        jnp.broadcast_to(info[None], (n_z,) + info.shape), "z", split_axis=0, concat_axis=0, tiled=True
    )

    full_gate = jnp.concatenate(gather_x(w_gate[0]), axis=0)
    full_up = jnp.concatenate(gather_x(w_up[0]), axis=0)
    full_down = jnp.concatenate(gather_x(w_down[0]), axis=1)

    local = info[:, :top] - me_z * (n_w * CAP)
    here = (local >= 0) & (local < n_w * CAP)
    source = jnp.arange(n_z, dtype=jnp.int32)[:, None, None]
    place = jnp.where(here, (local // CAP) * group + source * CAP + local % CAP, -1)
    gain = info[:, top : 2 * top].astype(f32) / 256.0
    flat = lambda a, k: a[:, k].reshape(1, n_z * tok)
    row_ids = jnp.arange(slots, dtype=jnp.int32)[:, None]
    hits = [row_ids == flat(place, k) for k in range(top)]
    pick = sum(jnp.where(h, 1.0, 0.0) for h in hits).astype(bf16)
    pick_gain = sum(jnp.where(h, flat(gain, k), 0.0) for k, h in enumerate(hits)).astype(bf16)

    def forward(chunk, select):
        column = lax.all_gather(chunk, "z", axis=0, tiled=True)
        chosen = dot(select, column).astype(bf16).reshape(n_w, group, -1)
        return lax.all_to_all(chosen, "w", split_axis=0, concat_axis=0, tiled=True).reshape(slots, -1)

    def backward(chunk):
        got = lax.all_to_all(
            chunk.reshape(n_w, group, -1), "w", split_axis=0, concat_axis=0, tiled=True
        ).reshape(slots, -1)
        column = dot(pick, got, ROWS0).astype(bf16)
        return lax.psum_scatter(column, "z", scatter_dimension=0, tiled=True)

    start = me_x * quarter
    rows = forward(roll_cols(tokens, start), pick)
    turned = roll_cols(out_grad, start)
    half = width // 2
    zgrad = [forward(turned[:, :half], pick_gain), forward(turned[:, half:], pick_gain)]

    pre_gate = dot(rows, full_gate)
    pre_up = dot(rows, full_up)
    sigma = jax.nn.sigmoid(pre_gate)
    swish = pre_gate * sigma
    hidden = (swish * pre_up).astype(bf16)
    grad_hidden = dot(zgrad[0], full_down[:, :half], COLS1) + dot(zgrad[1], full_down[:, half:], COLS1)
    grad_gate = (grad_hidden * pre_up * sigma * (1.0 + pre_gate * (1.0 - sigma))).astype(bf16)
    grad_up = (grad_hidden * swish).astype(bf16)

    parts = []
    for h in range(2):
        cols = slice(h * half, (h + 1) * half)
        back = dot(grad_gate, full_gate[cols], COLS1) + dot(grad_up, full_up[cols], COLS1)
        parts.append(backward(back.astype(bf16)))
    turned_back = jnp.concatenate(parts, axis=1)
    grad_tokens = roll_cols(turned_back, (n_x - me_x) % n_x * quarter)

    def cols_of(v, q):
        return v[:, q * quarter : (q + 1) * quarter]

    zcols = lambda q: cols_of(zgrad[q // 2], q % 2)
    out_gate = scatter_x(lambda q: dot(cols_of(rows, q), grad_gate, ROWS0))
    out_up = scatter_x(lambda q: dot(cols_of(rows, q), grad_up, ROWS0))
    out_down = scatter_x(lambda q: dot(hidden, zcols(q), ROWS0))
    return grad_tokens, out_gate, out_up, out_down


def solution(mesh):
    n_dp, n_expert = mesh.devices.shape
    inner = 8
    fine = Mesh(mesh.devices.reshape(n_dp, n_expert // inner, inner), ("x", "z", "w"))
    tok = P(("x", "z", "w"), None)
    by_rows = P(("z", "w"), "x", None)
    by_cols = P(("z", "w"), None, "x")
    return jax.shard_map(
        per_device,
        mesh=fine,
        in_specs=(tok, tok, tok, tok, by_rows, by_rows, by_cols),
        out_specs=(tok, by_rows, by_rows, by_cols),
        check_vma=False,
    )
```

```python
import jax
import jax.numpy as jnp
from jax import lax
from jax.experimental import pallas as pl
from jax.experimental.pallas import tpu as pltpu
from jax.sharding import Mesh, PartitionSpec as P

CAP = 9
ROWS0 = (((0,), (0,)), ((), ()))
COLS1 = (((1,), (1,)), ((), ()))
f32 = jnp.float32
bf16 = jnp.bfloat16


def shift(v, axis, step):
    n = lax.axis_size(axis)
    return lax.ppermute(v, axis, [(i, (i + step) % n) for i in range(n)])


def dot(a, b, dims=(((1,), (0,)), ((), ()))):
    return lax.dot_general(a, b, dims, preferred_element_type=f32)


def after(v, *others):
    return lax.optimization_barrier((v,) + others)[0]


def ring_z(low, high):
    n = lax.axis_size("z")
    far = n // 2
    lows, highs = [None] * n, [None] * n
    lows[0], highs[0] = low, high
    lu = ld = low
    hu = hd = high
    for s in range(1, far + 1):
        lu = lows[s] = shift(lu, "z", -1)
        if s < far:
            hu = highs[s] = shift(hu, "z", -1)
            ld = lows[n - s] = shift(ld, "z", 1)
        hd = highs[n - s] = shift(hd, "z", 1)
    return lows, highs


def pick_kernel(n, per_half, select, *refs):
    out = refs[-1]
    block = pl.program_id(0)

    def write(pieces):
        column = jnp.concatenate([p[...] for p in pieces], axis=0)
        out[...] = jnp.dot(select[...], column, preferred_element_type=f32).astype(out.dtype)

    pl.when(block < per_half)(lambda: write(refs[:n]))
    pl.when(block >= per_half)(lambda: write(refs[n : 2 * n]))


def pick_rows(select, lows, highs):
    n = len(lows)
    slots, depth = select.shape
    rows, half = lows[0].shape
    wide = 512
    per_half = half // wide
    low_spec = pl.BlockSpec((rows, wide), lambda j: (0, jnp.minimum(j, per_half - 1)))
    high_spec = pl.BlockSpec((rows, wide), lambda j: (0, jnp.maximum(j - per_half, 0)))
    return pl.pallas_call(
        lambda *refs: pick_kernel(n, per_half, *refs),
        grid=(2 * per_half,),
        in_specs=[pl.BlockSpec((slots, depth), lambda j: (0, 0))] + [low_spec] * n + [high_spec] * n,
        out_specs=pl.BlockSpec((slots, wide), lambda j: (0, j)),
        out_shape=jax.ShapeDtypeStruct((slots, 2 * half), bf16),
        compiler_params=pltpu.CompilerParams(vmem_limit_bytes=32 * 1024 * 1024),
        cost_estimate=pl.CostEstimate(
            flops=4 * slots * depth * half, bytes_accessed=4 * (slots + depth) * half, transcendentals=0
        ),
    )(select, *lows, *highs)


def halves(v):
    middle = v.shape[0] // 2
    return v[:middle], v[middle:]


def per_device(tokens, out_grad, routes, levels, w_gate, w_up, w_down):
    tok, width = tokens.shape
    top = routes.shape[1]
    n_z, n_w, n_x = lax.axis_size("z"), lax.axis_size("w"), lax.axis_size("x")
    n_expert = n_z * n_w
    quarter = width // n_x
    half = width // 2
    ff = w_gate.shape[2]
    me_x, me_z = lax.axis_index("x"), lax.axis_index("z")
    group = n_z * CAP
    slots = n_w * group

    full_pair = lax.all_gather(jnp.concatenate([w_gate[0], w_up[0]], axis=1), "x", axis=0, tiled=True)
    full_down = lax.all_gather(w_down[0], "x", axis=1, tiled=True)

    named = [(routes[:, k : k + 1] == jnp.arange(n_expert)[None, :]).astype(f32) for k in range(top)]
    lower = (jnp.arange(tok)[:, None] > jnp.arange(tok)[None, :]).astype(bf16)
    before = dot(lower, sum(named).astype(bf16))
    rank = [jnp.sum(before * m, axis=1).astype(jnp.int32) for m in named]
    info = jnp.stack(
        [routes[:, k] * CAP + rank[k] for k in range(top)]
        + [levels[:, k] for k in range(top)]
        + [jnp.zeros((tok,), jnp.int32)] * (8 - 2 * top),
        axis=0,
    )
    info = lax.all_to_all(
        jnp.broadcast_to(info[None], (n_z,) + info.shape), "z", split_axis=0, concat_axis=0, tiled=True
    )
    t_low, t_high = ring_z(tokens[:, :half], tokens[:, half:])
    out_grad = after(out_grad, t_low[n_z // 2 - 1], t_high[n_z // 2 + 1])
    g_low, g_high = ring_z(out_grad[:, :half], out_grad[:, half:])
    info = after(info, t_low[2], t_high[2])

    info = lax.dynamic_slice(jnp.concatenate([info, info], axis=0), (me_z, 0, 0), info.shape)

    local = info[:, :top] - me_z * (n_w * CAP)
    here = (local >= 0) & (local < n_w * CAP)
    source = jnp.arange(n_z, dtype=jnp.int32)[:, None, None]
    place = jnp.where(here, (local // CAP) * group + source * CAP + local % CAP, -1)
    gain = info[:, top : 2 * top].astype(f32) / 256.0
    flat = lambda a, k: a[:, k].reshape(1, n_z * tok)
    row_ids = jnp.arange(slots, dtype=jnp.int32)[:, None]
    hits = [row_ids == flat(place, k) for k in range(top)]
    pick = sum(jnp.where(h, 1.0, 0.0) for h in hits).astype(bf16)
    pick_gain = sum(jnp.where(h, flat(gain, k), 0.0) for k, h in enumerate(hits)).astype(bf16)
    home = lax.dynamic_slice(jnp.concatenate([place, place], axis=0), (n_z - me_z, 0, 0), place.shape)
    spread = sum(
        jnp.where(flat(home, k).reshape(-1, 1) == row_ids.reshape(1, -1), 1.0, 0.0) for k in range(top)
    ).astype(bf16)

    def exchange(v):
        return lax.all_to_all(v.reshape(n_w, group, -1), "w", split_axis=0, concat_axis=0, tiled=True).reshape(slots, -1)

    zgrad_sent = pick_rows(pick_gain, g_low, g_high)
    t_low, t_high = after((t_low, t_high), g_low[1], g_high[n_z - 1])
    rows = exchange(pick_rows(pick, t_low, t_high))
    zgrad = exchange(zgrad_sent)

    pre = dot(rows, full_pair)
    pre_gate, pre_up = pre[:, :ff], pre[:, ff:]
    sigma = jax.nn.sigmoid(pre_gate)
    swish = pre_gate * sigma
    hidden = (swish * pre_up).astype(bf16)
    grad_hidden = dot(zgrad, full_down, COLS1)
    grad_gate = (grad_hidden * pre_up * sigma * (1.0 + pre_gate * (1.0 - sigma))).astype(bf16)
    grad_up = (grad_hidden * swish).astype(bf16)
    grad_pair = jnp.concatenate([grad_gate, grad_up], axis=1)

    back = exchange(dot(grad_pair, full_pair, COLS1).astype(bf16))

    def cols_of(v, q):
        return lax.dynamic_slice(v, (0, (me_x + q) % n_x * quarter), (slots, quarter))

    pair_term = lambda q: dot(cols_of(rows, q), grad_pair, ROWS0)
    down_term = lambda q: dot(hidden, cols_of(zgrad, q), ROWS0)

    def first_sends(term):
        far_a, far_b = halves(term(2).astype(bf16))
        via_right, via_left = shift(far_a, "x", 1), shift(far_b, "x", -1)
        right_a, right_b = halves(term(1))
        left_a, left_b = halves(term(3))
        from_left_b = shift(right_b.astype(bf16), "x", 1)
        from_right_a = shift(left_a.astype(bf16), "x", -1)
        right_a = (right_a + via_right.astype(f32)).astype(bf16)
        left_b = (left_b + via_left.astype(f32)).astype(bf16)
        return right_a, left_b, from_left_b, from_right_a

    def last_sends(term, right_a, left_b, from_left_b, from_right_a):
        from_left_a = shift(right_a, "x", 1)
        from_right_b = shift(left_b, "x", -1)
        own_a, own_b = halves(term(0))
        own_a = own_a + from_left_a.astype(f32) + from_right_a.astype(f32)
        own_b = own_b + from_left_b.astype(f32) + from_right_b.astype(f32)
        return jnp.concatenate([own_a, own_b], axis=0).astype(bf16)

    pair_first = first_sends(pair_term)
    down_first = first_sends(down_term)
    back = after(back, *pair_first)

    column = dot(spread, back).astype(bf16)
    grad_tokens = lax.psum_scatter(column, "z", scatter_dimension=0, tiled=True)

    out_pair = last_sends(pair_term, *pair_first)
    out_down = last_sends(down_term, *down_first)
    return grad_tokens, out_pair[None, :, :ff], out_pair[None, :, ff:], out_down[None]


def solution(mesh):
    n_dp, n_expert = mesh.devices.shape
    inner = 8
    fine = Mesh(mesh.devices.reshape(n_dp, n_expert // inner, inner), ("x", "z", "w"))
    tok = P(("x", "z", "w"), None)
    by_rows = P(("z", "w"), "x", None)
    by_cols = P(("z", "w"), None, "x")
    return jax.shard_map(
        per_device,
        mesh=fine,
        in_specs=(tok, tok, tok, tok, by_rows, by_rows, by_cols),
        out_specs=(tok, by_rows, by_rows, by_cols),
        check_vma=False,
    )
```

```python
import jax
import jax.numpy as jnp
from jax import lax
from jax.experimental import pallas as pl
from jax.experimental.pallas import tpu as pltpu
from jax.sharding import Mesh, PartitionSpec as P

CAP = 9
ROWS0 = (((0,), (0,)), ((), ()))
COLS1 = (((1,), (1,)), ((), ()))
f32 = jnp.float32
bf16 = jnp.bfloat16


def shift(v, axis, step):
    n = lax.axis_size(axis)
    return lax.ppermute(v, axis, [(i, (i + step) % n) for i in range(n)])


def dot(a, b, dims=(((1,), (0,)), ((), ()))):
    return lax.dot_general(a, b, dims, preferred_element_type=f32)


def after(v, *others):
    return lax.optimization_barrier((v,) + others)[0]


def ring_z(piece, up_last, gate=None):
    n = lax.axis_size("z")
    far = n // 2
    pieces = [None] * n
    pieces[0] = up = down = piece
    for s in range(1, far):
        pieces[s], pieces[n - s] = shift(up, "z", -1), shift(down, "z", 1)
        up, down = pieces[s], pieces[n - s] = lax.optimization_barrier((pieces[s], pieces[n - s]))
        if s == 2 and gate is not None:
            up, down = after((up, down), gate)
    pieces[far] = shift(up, "z", -1) if up_last else shift(down, "z", 1)
    return pieces


def pick_kernel(n, per_half, select, *refs):
    out = refs[-1]
    block = pl.program_id(0)

    def write(pieces):
        column = jnp.concatenate([p[...] for p in pieces], axis=0)
        out[...] = jnp.dot(select[...], column, preferred_element_type=f32).astype(out.dtype)

    pl.when(block < per_half)(lambda: write(refs[:n]))
    pl.when(block >= per_half)(lambda: write(refs[n : 2 * n]))


def pick_rows(select, lows, highs, weight=1):
    n = len(lows)
    slots, depth = select.shape
    rows, half = lows[0].shape
    wide = 512
    per_half = half // wide
    low_spec = pl.BlockSpec((rows, wide), lambda j: (0, jnp.minimum(j, per_half - 1)))
    high_spec = pl.BlockSpec((rows, wide), lambda j: (0, jnp.maximum(j - per_half, 0)))
    return pl.pallas_call(
        lambda *refs: pick_kernel(n, per_half, *refs),
        grid=(2 * per_half,),
        in_specs=[pl.BlockSpec((slots, depth), lambda j: (0, 0))] + [low_spec] * n + [high_spec] * n,
        out_specs=pl.BlockSpec((slots, wide), lambda j: (0, j)),
        out_shape=jax.ShapeDtypeStruct((slots, 2 * half), bf16),
        compiler_params=pltpu.CompilerParams(vmem_limit_bytes=32 * 1024 * 1024),
        cost_estimate=pl.CostEstimate(
            flops=4 * weight * slots * depth * half,
            bytes_accessed=4 * weight * (slots + depth) * half,
            transcendentals=0,
        ),
    )(select, *lows, *highs)


def spread_kernel(select, rows, out):
    out[...] = jnp.dot(select[...], rows[...], preferred_element_type=f32).astype(out.dtype)


def spread_rows(select, rows):
    tall, depth = select.shape
    width = rows.shape[1]
    wide = 512
    return pl.pallas_call(
        spread_kernel,
        grid=(width // wide,),
        in_specs=[pl.BlockSpec((tall, depth), lambda j: (0, 0)), pl.BlockSpec((depth, wide), lambda j: (0, j))],
        out_specs=pl.BlockSpec((tall, wide), lambda j: (0, j)),
        out_shape=jax.ShapeDtypeStruct((tall, width), bf16),
        compiler_params=pltpu.CompilerParams(vmem_limit_bytes=32 * 1024 * 1024),
        cost_estimate=pl.CostEstimate(
            flops=2 * tall * depth * width, bytes_accessed=2 * (tall + depth) * width, transcendentals=0
        ),
    )(select, rows)


def total_kernel(own, from_left, from_right, *outs):
    total = own[...] + from_left[...].astype(f32) + from_right[...].astype(f32)
    wide = total.shape[1] // len(outs)
    for n, out in enumerate(outs):
        out[...] = total[:, n * wide : (n + 1) * wide].astype(out.dtype)


def total_of(own, from_left, from_right, parts, weight):
    tall, wide = own.shape
    rows = tall // 4
    spec = pl.BlockSpec((rows, wide), lambda j: (j, 0))
    part = pl.BlockSpec((rows, wide // parts), lambda j: (j, 0))
    return pl.pallas_call(
        total_kernel,
        grid=(4,),
        in_specs=[spec] * 3,
        out_specs=[part] * parts,
        out_shape=[jax.ShapeDtypeStruct((tall, wide // parts), bf16)] * parts,
        compiler_params=pltpu.CompilerParams(vmem_limit_bytes=32 * 1024 * 1024),
        cost_estimate=pl.CostEstimate(
            flops=weight * 2 * tall * wide, bytes_accessed=weight * 10 * tall * wide, transcendentals=0
        ),
    )(own, from_left, from_right)


def halves(v):
    middle = v.shape[0] // 2
    return v[:middle], v[middle:]


def per_device(tokens, out_grad, routes, levels, w_gate, w_up, w_down):
    tok, width = tokens.shape
    top = routes.shape[1]
    n_z, n_w, n_x = lax.axis_size("z"), lax.axis_size("w"), lax.axis_size("x")
    n_expert = n_z * n_w
    quarter = width // n_x
    half = width // 2
    ff = w_gate.shape[2]
    me_x, me_z = lax.axis_index("x"), lax.axis_index("z")
    group = n_z * CAP
    slots = n_w * group

    full_pair = lax.all_gather(jnp.concatenate([w_gate[0], w_up[0]], axis=1), "x", axis=0, tiled=True)
    full_down = lax.all_gather(w_down[0], "x", axis=1, tiled=True)

    named = [(routes[:, k : k + 1] == jnp.arange(n_expert)[None, :]).astype(f32) for k in range(top)]
    lower = (jnp.arange(tok)[:, None] > jnp.arange(tok)[None, :]).astype(bf16)
    before = dot(lower, sum(named).astype(bf16))
    rank = [jnp.sum(before * m, axis=1).astype(jnp.int32) for m in named]
    info = jnp.stack(
        [routes[:, k] * CAP + rank[k] for k in range(top)]
        + [levels[:, k] for k in range(top)]
        + [jnp.zeros((tok,), jnp.int32)] * (8 - 2 * top),
        axis=0,
    )
    info = lax.all_to_all(
        jnp.broadcast_to(info[None], (n_z,) + info.shape), "z", split_axis=0, concat_axis=0, tiled=True
    )
    t_low, t_high = ring_z(tokens[:, :half], True), ring_z(tokens[:, half:], False, info)
    out_grad = after(out_grad, t_low[n_z // 2 - 1], t_high[n_z // 2 - 1])
    g_low, g_high = ring_z(out_grad[:, :half], True), ring_z(out_grad[:, half:], False)

    info = lax.dynamic_slice(jnp.concatenate([info, info], axis=0), (me_z, 0, 0), info.shape)

    local = info[:, :top] - me_z * (n_w * CAP)
    here = (local >= 0) & (local < n_w * CAP)
    source = jnp.arange(n_z, dtype=jnp.int32)[:, None, None]
    place = jnp.where(here, (local // CAP) * group + source * CAP + local % CAP, -1)
    gain = info[:, top : 2 * top].astype(f32) / 256.0
    flat = lambda a, k: a[:, k].reshape(1, n_z * tok)
    row_ids = jnp.arange(slots, dtype=jnp.int32)[:, None]
    hits = [row_ids == flat(place, k) for k in range(top)]
    pick = sum(jnp.where(h, 1.0, 0.0) for h in hits).astype(bf16)
    pick_gain = sum(jnp.where(h, flat(gain, k), 0.0) for k, h in enumerate(hits)).astype(bf16)
    home = lax.dynamic_slice(jnp.concatenate([place, place], axis=0), (n_z - me_z, 0, 0), place.shape)
    spread = sum(
        jnp.where(flat(home, k).reshape(-1, 1) == row_ids.reshape(1, -1), 1.0, 0.0) for k in range(top)
    ).astype(bf16)

    def exchange(v):
        return lax.all_to_all(v.reshape(n_w, group, -1), "w", split_axis=0, concat_axis=0, tiled=True).reshape(slots, -1)

    zgrad_sent = pick_rows(pick_gain, g_low, g_high, 5)
    rows = exchange(pick_rows(pick, t_low, t_high))
    zgrad = exchange(zgrad_sent)

    pre = dot(rows, full_pair)
    pre_gate, pre_up = pre[:, :ff], pre[:, ff:]
    sigma = jax.nn.sigmoid(pre_gate)
    swish = pre_gate * sigma
    hidden = (swish * pre_up).astype(bf16)
    grad_hidden = dot(zgrad, full_down, COLS1)
    grad_gate = (grad_hidden * pre_up * sigma * (1.0 + pre_gate * (1.0 - sigma))).astype(bf16)
    grad_up = (grad_hidden * swish).astype(bf16)
    grad_pair = jnp.concatenate([grad_gate, grad_up], axis=1)

    back = dot(grad_pair, full_pair, COLS1).astype(bf16)
    back = exchange(back)

    def cols_of(v, q):
        return lax.dynamic_slice(v, (0, (me_x + q) % n_x * quarter), (slots, quarter))

    pair_term = lambda q: dot(cols_of(rows, q), grad_pair, ROWS0)
    down_term = lambda q: dot(hidden, cols_of(zgrad, q), ROWS0)

    def send_far(term):
        far_a, far_b = halves(term(2).astype(bf16))
        return shift(far_a, "x", 1), shift(far_b, "x", -1)

    def toward(term, via_right, via_left):
        right, left = term(1), term(3)
        middle = right.shape[0] // 2
        right = jnp.concatenate([right[:middle] + via_right.astype(f32), right[middle:]], axis=0)
        left = jnp.concatenate([left[:middle], left[middle:] + via_left.astype(f32)], axis=0)
        return right.astype(bf16), left.astype(bf16)

    def send_near(right, left):
        return shift(right, "x", 1), shift(left, "x", -1)

    pair_far, down_far = send_far(pair_term), send_far(down_term)
    pair_near = toward(pair_term, *pair_far)
    back = after(back, pair_near, down_far)
    pair_in = send_near(*pair_near)
    down_in = send_near(*toward(down_term, *down_far))

    column = spread_rows(spread, back)
    grad_tokens = lax.psum_scatter(column, "z", scatter_dimension=0, tiled=True)
    out_gate, out_up = total_of(pair_term(0), *pair_in, 2, 1)
    (out_down,) = total_of(down_term(0), *down_in, 1, 1)
    return grad_tokens, out_gate[None], out_up[None], out_down[None]


def solution(mesh):
    n_dp, n_expert = mesh.devices.shape
    inner = 8
    fine = Mesh(mesh.devices.reshape(n_dp, n_expert // inner, inner), ("x", "z", "w"))
    tok = P(("x", "z", "w"), None)
    by_rows = P(("z", "w"), "x", None)
    by_cols = P(("z", "w"), None, "x")
    return jax.shard_map(
        per_device,
        mesh=fine,
        in_specs=(tok, tok, tok, tok, by_rows, by_rows, by_cols),
        out_specs=(tok, by_rows, by_rows, by_cols),
        check_vma=False,
    )
```

```python
import functools

import jax
import jax.numpy as jnp
from jax import lax
from jax.experimental import pallas as pl
from jax.experimental.pallas import tpu as pltpu
from jax.sharding import Mesh, PartitionSpec as P

CAP = 9
ROWS0 = (((0,), (0,)), ((), ()))
COLS1 = (((1,), (1,)), ((), ()))
f32 = jnp.float32
bf16 = jnp.bfloat16


def shift(v, axis, step):
    n = lax.axis_size(axis)
    return lax.ppermute(v, axis, [(i, (i + step) % n) for i in range(n)])


def dot(a, b, dims=(((1,), (0,)), ((), ()))):
    return lax.dot_general(a, b, dims, preferred_element_type=f32)


def after(v, *others):
    return lax.optimization_barrier((v,) + others)[0]


def ring_z(piece, up_last, gate=None):
    n = lax.axis_size("z")
    far = n // 2
    pieces = [None] * n
    pieces[0] = up = down = piece
    for s in range(1, far):
        pieces[s], pieces[n - s] = shift(up, "z", -1), shift(down, "z", 1)
        up, down = pieces[s], pieces[n - s] = lax.optimization_barrier((pieces[s], pieces[n - s]))
        if s == 2 and gate is not None:
            up, down = after((up, down), gate)
    pieces[far] = shift(up, "z", -1) if up_last else shift(down, "z", 1)
    return pieces


def choose_kernel(per_half, n_out, select, *refs):
    pieces, outs = refs[:-n_out], refs[-n_out:]
    block = pl.program_id(0)

    def write(part):
        column = jnp.concatenate([p[...] for p in part], axis=0)
        chosen = jnp.dot(select[...], column, preferred_element_type=f32).astype(bf16)
        rows = chosen.shape[0] // n_out
        for n, out in enumerate(outs):
            out[...] = chosen[n * rows : (n + 1) * rows]

    if per_half is None:
        write(pieces)
    else:
        pl.when(block < per_half)(lambda: write(pieces[: len(pieces) // 2]))
        pl.when(block >= per_half)(lambda: write(pieces[len(pieces) // 2 :]))


def choose(select, pieces, highs=(), n_out=1, vmem=32):
    slots, depth = select.shape
    wide, width = 512, 2048
    per_half = width // wide // 2 if highs else None
    low = (lambda j: jnp.minimum(j, per_half - 1)) if highs else (lambda j: j)
    high = lambda j: jnp.maximum(j - per_half, 0)
    return pl.pallas_call(
        functools.partial(choose_kernel, per_half, n_out),
        grid=(width // wide,),
        in_specs=[pl.BlockSpec((slots, depth), lambda j: (0, 0))]
        + [pl.BlockSpec((p.shape[0], wide), lambda j: (0, low(j))) for p in pieces]
        + [pl.BlockSpec((p.shape[0], wide), lambda j: (0, high(j))) for p in highs],
        out_specs=[pl.BlockSpec((slots // n_out, wide), lambda j: (0, j))] * n_out,
        out_shape=[jax.ShapeDtypeStruct((slots // n_out, width), bf16)] * n_out,
        compiler_params=pltpu.CompilerParams(vmem_limit_bytes=vmem * 1024 * 1024),
        cost_estimate=pl.CostEstimate(
            flops=2 * slots * depth * width,
            bytes_accessed=2 * (slots + depth) * width,
            transcendentals=0,
        ),
    )(select, *pieces, *highs)


def total_kernel(own, from_left, from_right, *outs):
    total = own[...] + from_left[...].astype(f32) + from_right[...].astype(f32)
    wide = total.shape[1] // len(outs)
    for n, out in enumerate(outs):
        out[...] = total[:, n * wide : (n + 1) * wide].astype(out.dtype)


def total_of(own, from_left, from_right, parts, weight):
    tall, wide = own.shape
    rows = tall // 4
    spec = pl.BlockSpec((rows, wide), lambda j: (j, 0))
    part = pl.BlockSpec((rows, wide // parts), lambda j: (j, 0))
    return pl.pallas_call(
        total_kernel,
        grid=(4,),
        in_specs=[spec] * 3,
        out_specs=[part] * parts,
        out_shape=[jax.ShapeDtypeStruct((tall, wide // parts), bf16)] * parts,
        compiler_params=pltpu.CompilerParams(vmem_limit_bytes=32 * 1024 * 1024),
        cost_estimate=pl.CostEstimate(
            flops=2 * tall * wide, bytes_accessed=weight * 10 * tall * wide, transcendentals=0
        ),
    )(own, from_left, from_right)


def halves(v):
    middle = v.shape[0] // 2
    return v[:middle], v[middle:]


def per_device(tokens, out_grad, routes, levels, w_gate, w_up, w_down):
    tok, width = tokens.shape
    top = routes.shape[1]
    n_x, n_z, n_y, n_c = [lax.axis_size(axis) for axis in ("x", "z", "y", "c")]
    me_x, me_z, me_y, me_c = [lax.axis_index(axis) for axis in ("x", "z", "y", "c")]
    n_w = n_y * n_c
    n_expert = n_z * n_w
    quarter = width // n_x
    half = width // 2
    ff = w_gate.shape[2]
    group = n_z * CAP
    slots = n_w * group
    block = -(-n_y * CAP // 8) * 8
    sent = n_z * n_c * block
    hop = sent // n_w

    full_pair = lax.all_gather(jnp.concatenate([w_gate[0], w_up[0]], axis=1), "x", axis=0, tiled=True)
    full_down = lax.all_gather(w_down[0], "x", axis=1, tiled=True)

    named = [(routes[:, k : k + 1] == jnp.arange(n_expert)[None, :]).astype(f32) for k in range(top)]
    lower = (jnp.arange(tok)[:, None] > jnp.arange(tok)[None, :]).astype(bf16)
    before = dot(lower, sum(named).astype(bf16))
    rank = [jnp.sum(before * m, axis=1).astype(jnp.int32) for m in named]
    info = jnp.stack(
        [routes[:, k] * CAP + rank[k] for k in range(top)] + [jnp.zeros((tok,), jnp.int32)] * (8 - top), axis=0
    )
    info = lax.all_to_all(
        jnp.broadcast_to(info[None], (n_z,) + info.shape), "z", split_axis=0, concat_axis=0, tiled=True
    )
    t_low, t_high = ring_z(tokens[:, :half], True), ring_z(tokens[:, half:], False, info)

    marks = jnp.concatenate([routes, jnp.stack(rank, axis=1), levels], axis=1).astype(bf16)
    marks = jnp.pad(marks, ((0, 0), (0, 128 - 3 * top)))
    own_g = jnp.concatenate([out_grad, marks], axis=1)
    right_g, left_g = shift(own_g, "y", -1), shift(own_g, "y", 1)
    far_g = shift(halves(right_g)[0], "y", -1), shift(halves(left_g)[1], "y", 1)
    row_g = [own_g, right_g, *far_g, left_g]
    sent_ids = jnp.arange(sent, dtype=jnp.int32)[:, None]
    slot_ids = jnp.arange(slots, dtype=jnp.int32)

    marks = jnp.concatenate([piece[:, width : width + 3 * top] for piece in row_g], axis=0).astype(jnp.int32).T
    expert, rank, level = marks[:top], marks[top : 2 * top], marks[2 * top :]
    source_y = (me_y + jnp.arange(n_y * tok, dtype=jnp.int32) // tok) % n_y
    place = expert // n_w * n_c + expert % n_c
    place = jnp.where(expert // n_c % n_y == me_y, place * block + source_y * CAP + rank, -1)
    gain = level.astype(f32) / 256.0
    pick_gain = sum(jnp.where(sent_ids == place[k : k + 1], gain[k : k + 1], 0.0) for k in range(top)).astype(bf16)

    local = info[:, :top] - me_z * (n_w * CAP)
    here = (local >= 0) & (local < n_w * CAP)
    target, nth = local // CAP, local % CAP
    source_z = jnp.arange(n_z, dtype=jnp.int32)[:, None, None]
    turn = lambda a: lax.dynamic_slice(jnp.concatenate([a, a], axis=0), (me_z, 0, 0), a.shape)
    flat = lambda a, k: a[:, k].reshape(1, n_z * tok)
    away = (target // n_c - me_y + n_y) % n_y * n_c + (target % n_c + me_c) % n_c
    place = turn(jnp.where(here, away * hop + source_z * CAP + nth, -1))
    pick = sum(jnp.where(sent_ids == flat(place, k), 1.0, 0.0) for k in range(top)).astype(bf16)
    home = jnp.where(here, target * group + source_z * CAP + nth, -1)
    spread = sum(jnp.where(flat(home, k).reshape(-1, 1) == slot_ids[None, :], 1.0, 0.0) for k in range(top)).astype(bf16)

    came = jnp.arange(sent, dtype=jnp.int32)[None, :]
    from_y = (me_y - came // hop // n_c + n_y) % n_y
    from_c = (came // hop + me_c) % n_c
    meet = (from_y * n_c + from_c) * group + came % hop
    meet = ((slot_ids[:, None] == meet) & (came % hop < group)).astype(bf16)
    source_w, source_z, nth = slot_ids // group, slot_ids % group // CAP, slot_ids % CAP
    order = (source_z * n_c + source_w % n_c) * block + source_w // n_c * CAP + nth
    order = (order[:, None] == came).astype(bf16)

    (zgrad_sent,) = choose(pick_gain, row_g)
    zgrad_sent = after(zgrad_sent, t_low[n_z // 2], t_high[n_z // 2])
    zgrad = lax.all_to_all(
        zgrad_sent.reshape(n_z * n_c, block, width), ("z", "c"), split_axis=0, concat_axis=0, tiled=True
    ).reshape(sent, width)
    rows = list(choose(pick, t_low, t_high, n_w, 56))
    for n in range(1, n_w):
        dy, dc = n // n_c, n % n_c
        route = [(y * n_c + c, (y + dy) % n_y * n_c + (c + dc) % n_c) for y in range(n_y) for c in range(n_c)]
        rows[n] = lax.ppermute(rows[n], ("y", "c"), route)
    (rows,) = choose(meet, rows)

    def exchange(v):
        v = v.reshape(n_w, group, -1)
        return lax.all_to_all(v, ("y", "c"), split_axis=0, concat_axis=0, tiled=True).reshape(slots, -1)

    pre = dot(rows, full_pair)
    (zgrad,) = choose(order, [after(zgrad, pre)])
    pre_gate, pre_up = pre[:, :ff], pre[:, ff:]
    sigma = jax.nn.sigmoid(pre_gate)
    swish = pre_gate * sigma
    hidden = (swish * pre_up).astype(bf16)
    grad_hidden = dot(zgrad, full_down, COLS1)
    grad_gate = (grad_hidden * pre_up * sigma * (1.0 + pre_gate * (1.0 - sigma))).astype(bf16)
    grad_up = (grad_hidden * swish).astype(bf16)
    grad_pair = jnp.concatenate([grad_gate, grad_up], axis=1)

    back = dot(grad_pair, full_pair, COLS1).astype(bf16)
    back = exchange(back)

    def cols_of(v, q):
        return lax.dynamic_slice(v, (0, (me_x + q) % n_x * quarter), (slots, quarter))

    pair_term = lambda q: dot(cols_of(rows, q), grad_pair, ROWS0)
    down_term = lambda q: dot(hidden, cols_of(zgrad, q), ROWS0)

    def send_far(term):
        far_a, far_b = halves(term(2).astype(bf16))
        return shift(far_a, "x", 1), shift(far_b, "x", -1)

    def toward(term, via_right, via_left):
        right, left = term(1), term(3)
        middle = right.shape[0] // 2
        right = jnp.concatenate([right[:middle] + via_right.astype(f32), right[middle:]], axis=0)
        left = jnp.concatenate([left[:middle], left[middle:] + via_left.astype(f32)], axis=0)
        return right.astype(bf16), left.astype(bf16)

    def send_near(right, left):
        return shift(right, "x", 1), shift(left, "x", -1)

    pair_far, down_far = send_far(pair_term), send_far(down_term)
    pair_near = toward(pair_term, *pair_far)
    back = after(back, pair_near, down_far)
    pair_in = send_near(*pair_near)
    down_in = send_near(*toward(down_term, *down_far))

    (column,) = choose(spread, [back])
    grad_tokens = lax.psum_scatter(column, "z", scatter_dimension=0, tiled=True)
    out_gate, out_up = total_of(pair_term(0), *pair_in, 2, 1)
    (out_down,) = total_of(down_term(0), *down_in, 1, 1)
    return grad_tokens, out_gate[None], out_up[None], out_down[None]


def solution(mesh):
    n_dp, n_expert = mesh.devices.shape
    inner = 8
    fine = Mesh(mesh.devices.reshape(n_dp, n_expert // inner, inner // 2, 2), ("x", "z", "y", "c"))
    tok = P(("x", "z", "y", "c"), None)
    by_rows = P(("z", "y", "c"), "x", None)
    by_cols = P(("z", "y", "c"), None, "x")
    return jax.shard_map(
        per_device,
        mesh=fine,
        in_specs=(tok, tok, tok, tok, by_rows, by_rows, by_cols),
        out_specs=(tok, by_rows, by_rows, by_cols),
        check_vma=False,
    )
```

```python
import functools

import jax
import jax.numpy as jnp
from jax import lax
from jax.experimental import pallas as pl
from jax.experimental.pallas import tpu as pltpu
from jax.sharding import Mesh, PartitionSpec as P

CAP = 9
ROWS0 = (((0,), (0,)), ((), ()))
COLS1 = (((1,), (1,)), ((), ()))
f32 = jnp.float32
bf16 = jnp.bfloat16


def shift(v, axis, step):
    n = lax.axis_size(axis)
    return lax.ppermute(v, axis, [(i, (i + step) % n) for i in range(n)])


def dot(a, b, dims=(((1,), (0,)), ((), ()))):
    return lax.dot_general(a, b, dims, preferred_element_type=f32)


def after(v, *others):
    return lax.optimization_barrier((v,) + others)[0]


def ring_z(piece, up_last, gate=None):
    n = lax.axis_size("z")
    far = n // 2
    pieces = [None] * n
    pieces[0] = up = down = piece
    for s in range(1, far):
        pieces[s], pieces[n - s] = shift(up, "z", -1), shift(down, "z", 1)
        up, down = pieces[s], pieces[n - s] = lax.optimization_barrier((pieces[s], pieces[n - s]))
        if s == 2 and gate is not None:
            up, down = after((up, down), gate)
    pieces[far] = shift(up, "z", -1) if up_last else shift(down, "z", 1)
    return pieces


def choose_kernel(per_half, n_out, select, *refs):
    pieces, outs = refs[:-n_out], refs[-n_out:]
    block = pl.program_id(0)

    def write(part):
        column = jnp.concatenate([p[...] for p in part], axis=0)
        chosen = jnp.dot(select[...], column, preferred_element_type=f32).astype(bf16)
        rows = chosen.shape[0] // n_out
        for n, out in enumerate(outs):
            out[...] = chosen[n * rows : (n + 1) * rows]

    if per_half is None:
        write(pieces)
    else:
        pl.when(block < per_half)(lambda: write(pieces[: len(pieces) // 2]))
        pl.when(block >= per_half)(lambda: write(pieces[len(pieces) // 2 :]))


def choose(select, pieces, highs=(), n_out=1, vmem=16):
    slots, depth = select.shape
    wide, width = 512, 2048
    per_half = width // wide // 2 if highs else None
    low = (lambda j: jnp.minimum(j, per_half - 1)) if highs else (lambda j: j)
    high = lambda j: jnp.maximum(j - per_half, 0)
    return pl.pallas_call(
        functools.partial(choose_kernel, per_half, n_out),
        grid=(width // wide,),
        in_specs=[pl.BlockSpec((slots, depth), lambda j: (0, 0))]
        + [pl.BlockSpec((p.shape[0], wide), lambda j: (0, low(j))) for p in pieces]
        + [pl.BlockSpec((p.shape[0], wide), lambda j: (0, high(j))) for p in highs],
        out_specs=[pl.BlockSpec((slots // n_out, wide), lambda j: (0, j))] * n_out,
        out_shape=[jax.ShapeDtypeStruct((slots // n_out, width), bf16)] * n_out,
        compiler_params=pltpu.CompilerParams(vmem_limit_bytes=vmem * 1024 * 1024),
        cost_estimate=pl.CostEstimate(
            flops=2 * slots * depth * width,
            bytes_accessed=2 * (slots + depth) * width,
            transcendentals=0,
        ),
    )(select, *pieces, *highs)


def total_kernel(parts, *refs):
    outs = list(refs[3 * len(parts) :])
    for n, part in enumerate(parts):
        own, from_left, from_right = refs[3 * n : 3 * n + 3]
        total = own[...] + from_left[...].astype(f32) + from_right[...].astype(f32)
        wide = total.shape[1] // part
        for m in range(part):
            outs.pop(0)[...] = total[:, m * wide : (m + 1) * wide].astype(bf16)


def totals(owns, arrived, parts):
    in_specs, out_specs, out_shape, args = [], [], [], []
    for own, (from_left, from_right), part in zip(owns, arrived, parts):
        tall, wide = own.shape
        spec = pl.BlockSpec((tall // 4, wide), lambda j: (j, 0))
        in_specs += [spec] * 3
        out_specs += [pl.BlockSpec((tall // 4, wide // part), lambda j: (j, 0))] * part
        out_shape += [jax.ShapeDtypeStruct((tall, wide // part), bf16)] * part
        args += [own, from_left, from_right]
    return pl.pallas_call(
        lambda *refs: total_kernel(parts, *refs),
        grid=(4,),
        in_specs=in_specs,
        out_specs=out_specs,
        out_shape=out_shape,
        compiler_params=pltpu.CompilerParams(vmem_limit_bytes=24 * 1024 * 1024),
        cost_estimate=pl.CostEstimate(
            flops=2 * sum(own.size for own in owns),
            bytes_accessed=10 * sum(own.size for own in owns),
            transcendentals=0,
        ),
    )(*args)


def halves(v):
    middle = v.shape[0] // 2
    return v[:middle], v[middle:]


def per_device(tokens, out_grad, routes, levels, w_gate, w_up, w_down):
    tok, width = tokens.shape
    top = routes.shape[1]
    n_x, n_z, n_y, n_c = [lax.axis_size(axis) for axis in ("x", "z", "y", "c")]
    me_x, me_z, me_y, me_c = [lax.axis_index(axis) for axis in ("x", "z", "y", "c")]
    n_w = n_y * n_c
    n_expert = n_z * n_w
    quarter = width // n_x
    half = width // 2
    ff = w_gate.shape[2]
    group = n_z * CAP
    slots = n_w * group
    block = -(-n_y * CAP // 8) * 8
    sent = n_z * n_c * block
    hop = sent // n_w

    full_pair = lax.all_gather(jnp.concatenate([w_gate[0], w_up[0]], axis=1), "x", axis=0, tiled=True)
    full_down = lax.all_gather(w_down[0], "x", axis=1, tiled=True)

    named = [(routes[:, k : k + 1] == jnp.arange(n_expert)[None, :]).astype(f32) for k in range(top)]
    lower = (jnp.arange(tok)[:, None] > jnp.arange(tok)[None, :]).astype(bf16)
    before = dot(lower, sum(named).astype(bf16))
    rank = [jnp.sum(before * m, axis=1).astype(jnp.int32) for m in named]
    info = jnp.stack(
        [routes[:, k] * CAP + rank[k] for k in range(top)] + [jnp.zeros((tok,), jnp.int32)] * (8 - top), axis=0
    )
    info = lax.all_to_all(
        jnp.broadcast_to(info[None], (n_z,) + info.shape), "z", split_axis=0, concat_axis=0, tiled=True
    )
    t_low, t_high = ring_z(tokens[:, :half], True), ring_z(tokens[:, half:], False, info)

    marks = jnp.concatenate([routes, jnp.stack(rank, axis=1), levels], axis=1).astype(bf16)
    marks = jnp.pad(marks, ((0, 0), (0, 128 - 3 * top)))
    own_g = jnp.concatenate([out_grad, marks], axis=1)
    right_g, left_g = shift(own_g, "y", -1), shift(own_g, "y", 1)
    far_g = shift(halves(right_g)[0], "y", -1), shift(halves(left_g)[1], "y", 1)
    row_g = [own_g, right_g, *far_g, left_g]
    sent_ids = jnp.arange(sent, dtype=jnp.int32)[:, None]
    slot_ids = jnp.arange(slots, dtype=jnp.int32)

    marks = jnp.concatenate([piece[:, width : width + 3 * top] for piece in row_g], axis=0).astype(jnp.int32).T
    expert, rank, level = marks[:top], marks[top : 2 * top], marks[2 * top :]
    source_y = (me_y + jnp.arange(n_y * tok, dtype=jnp.int32) // tok) % n_y
    place = expert // n_w * n_c + expert % n_c
    place = jnp.where(expert // n_c % n_y == me_y, place * block + source_y * CAP + rank, -1)
    gain = level.astype(f32) / 256.0
    pick_gain = sum(jnp.where(sent_ids == place[k : k + 1], gain[k : k + 1], 0.0) for k in range(top)).astype(bf16)

    local = info[:, :top] - me_z * (n_w * CAP)
    here = (local >= 0) & (local < n_w * CAP)
    target, nth = local // CAP, local % CAP
    source_z = jnp.arange(n_z, dtype=jnp.int32)[:, None, None]
    turn = lambda a: lax.dynamic_slice(jnp.concatenate([a, a], axis=0), (me_z, 0, 0), a.shape)
    flat = lambda a, k: a[:, k].reshape(1, n_z * tok)
    away = (target // n_c - me_y + n_y) % n_y * n_c + (target % n_c + me_c) % n_c
    place = turn(jnp.where(here, away * hop + source_z * CAP + nth, -1))
    pick = sum(jnp.where(sent_ids == flat(place, k), 1.0, 0.0) for k in range(top)).astype(bf16)
    home = jnp.where(here, target * group + source_z * CAP + nth, -1)
    spread = sum(jnp.where(flat(home, k).reshape(-1, 1) == slot_ids[None, :], 1.0, 0.0) for k in range(top)).astype(bf16)

    came = jnp.arange(sent, dtype=jnp.int32)[None, :]
    from_y = (me_y - came // hop // n_c + n_y) % n_y
    from_c = (came // hop + me_c) % n_c
    meet = (from_y * n_c + from_c) * group + came % hop
    meet = ((slot_ids[:, None] == meet) & (came % hop < group)).astype(bf16)
    source_w, source_z, nth = slot_ids // group, slot_ids % group // CAP, slot_ids % CAP
    order = (source_z * n_c + source_w % n_c) * block + source_w // n_c * CAP + nth
    order = (order[:, None] == came).astype(bf16)

    (zgrad_sent,) = choose(pick_gain, row_g)
    zgrad_sent = after(zgrad_sent, t_low[n_z // 2], t_high[n_z // 2])
    zgrad = lax.all_to_all(
        zgrad_sent.reshape(n_z * n_c, block, width), ("z", "c"), split_axis=0, concat_axis=0, tiled=True
    ).reshape(sent, width)
    rows = list(choose(pick, t_low, t_high, n_w, 56))
    for n in range(1, n_w):
        dy, dc = n // n_c, n % n_c
        route = [(y * n_c + c, (y + dy) % n_y * n_c + (c + dc) % n_c) for y in range(n_y) for c in range(n_c)]
        rows[n] = lax.ppermute(rows[n], ("y", "c"), route)
    (rows,) = choose(meet, rows, vmem=8)

    def exchange(v):
        v = v.reshape(n_w, group, -1)
        return lax.all_to_all(v, ("y", "c"), split_axis=0, concat_axis=0, tiled=True).reshape(slots, -1)

    pre = dot(rows, full_pair)
    (zgrad,) = choose(order, [after(zgrad, pre)], vmem=8)
    pre_gate, pre_up = pre[:, :ff], pre[:, ff:]
    sigma = jax.nn.sigmoid(pre_gate)
    swish = pre_gate * sigma
    hidden = (swish * pre_up).astype(bf16)
    grad_hidden = dot(zgrad, full_down, COLS1)
    grad_gate = (grad_hidden * pre_up * sigma * (1.0 + pre_gate * (1.0 - sigma))).astype(bf16)
    grad_up = (grad_hidden * swish).astype(bf16)
    grad_pair = jnp.concatenate([grad_gate, grad_up], axis=1)

    back = dot(grad_pair, full_pair, COLS1).astype(bf16)
    back = exchange(back)

    def cols_of(v, q):
        return lax.dynamic_slice(v, (0, (me_x + q) % n_x * quarter), (slots, quarter))

    pair_term = lambda q: dot(cols_of(rows, q), grad_pair, ROWS0)
    down_term = lambda q: dot(hidden, cols_of(zgrad, q), ROWS0)

    def send_far(term):
        far_a, far_b = halves(term(2).astype(bf16))
        return shift(far_a, "x", 1), shift(far_b, "x", -1)

    def toward(term, via_right, via_left):
        right, left = term(1), term(3)
        middle = right.shape[0] // 2
        right = jnp.concatenate([right[:middle] + via_right.astype(f32), right[middle:]], axis=0)
        left = jnp.concatenate([left[:middle], left[middle:] + via_left.astype(f32)], axis=0)
        return right.astype(bf16), left.astype(bf16)

    def send_near(right, left):
        return shift(right, "x", 1), shift(left, "x", -1)

    pair_far, down_far = send_far(pair_term), send_far(down_term)
    pair_near = toward(pair_term, *pair_far)
    back = after(back, pair_near, down_far)
    pair_in = send_near(*pair_near)
    down_in = send_near(*toward(down_term, *down_far))

    (column,) = choose(spread, [back])
    grad_tokens = lax.psum_scatter(column, "z", scatter_dimension=0, tiled=True)
    out_gate, out_up, out_down = totals((pair_term(0), down_term(0)), (pair_in, down_in), (2, 1))
    return grad_tokens, out_gate[None], out_up[None], out_down[None]


def solution(mesh):
    n_dp, n_expert = mesh.devices.shape
    inner = 8
    fine = Mesh(mesh.devices.reshape(n_dp, n_expert // inner, inner // 2, 2), ("x", "z", "y", "c"))
    tok = P(("x", "z", "y", "c"), None)
    by_rows = P(("z", "y", "c"), "x", None)
    by_cols = P(("z", "y", "c"), None, "x")
    return jax.shard_map(
        per_device,
        mesh=fine,
        in_specs=(tok, tok, tok, tok, by_rows, by_rows, by_cols),
        out_specs=(tok, by_rows, by_rows, by_cols),
        check_vma=False,
    )
```

```python
import functools

import jax
import jax.numpy as jnp
from jax import lax
from jax.experimental import pallas as pl
from jax.experimental.pallas import tpu as pltpu
from jax.sharding import Mesh, PartitionSpec as P

CAP = 9
ROWS0 = (((0,), (0,)), ((), ()))
COLS1 = (((1,), (1,)), ((), ()))
f32 = jnp.float32
bf16 = jnp.bfloat16


def shift(v, axis, step):
    n = lax.axis_size(axis)
    return lax.ppermute(v, axis, [(i, (i + step) % n) for i in range(n)])


def dot(a, b, dims=(((1,), (0,)), ((), ()))):
    return lax.dot_general(a, b, dims, preferred_element_type=f32)


def after(v, *others):
    return lax.optimization_barrier((v,) + others)[0]


def ring_z(piece, up_last, gate=None):
    n = lax.axis_size("z")
    far = n // 2
    pieces = [None] * n
    pieces[0] = up = down = piece
    for s in range(1, far):
        pieces[s], pieces[n - s] = shift(up, "z", -1), shift(down, "z", 1)
        up, down = pieces[s], pieces[n - s] = lax.optimization_barrier((pieces[s], pieces[n - s]))
        if s == 2 and gate is not None:
            up, down = after((up, down), gate)
    pieces[far] = shift(up, "z", -1) if up_last else shift(down, "z", 1)
    return pieces


def choose_kernel(per_half, n_out, select, *refs):
    pieces, outs = refs[:-n_out], refs[-n_out:]
    block = pl.program_id(0)

    def write(part):
        column = jnp.concatenate([p[...] for p in part], axis=0)
        chosen = jnp.dot(select[...], column, preferred_element_type=f32).astype(bf16)
        rows = chosen.shape[0] // n_out
        for n, out in enumerate(outs):
            out[...] = chosen[n * rows : (n + 1) * rows]

    if per_half is None:
        write(pieces)
    else:
        pl.when(block < per_half)(lambda: write(pieces[: len(pieces) // 2]))
        pl.when(block >= per_half)(lambda: write(pieces[len(pieces) // 2 :]))


def choose(select, pieces, highs=(), n_out=1, vmem=16):
    slots, depth = select.shape
    wide, width = 512, 2048
    per_half = width // wide // 2 if highs else None
    low = (lambda j: jnp.minimum(j, per_half - 1)) if highs else (lambda j: j)
    high = lambda j: jnp.maximum(j - per_half, 0)
    return pl.pallas_call(
        functools.partial(choose_kernel, per_half, n_out),
        grid=(width // wide,),
        in_specs=[pl.BlockSpec((slots, depth), lambda j: (0, 0))]
        + [pl.BlockSpec((p.shape[0], wide), lambda j: (0, low(j))) for p in pieces]
        + [pl.BlockSpec((p.shape[0], wide), lambda j: (0, high(j))) for p in highs],
        out_specs=[pl.BlockSpec((slots // n_out, wide), lambda j: (0, j))] * n_out,
        out_shape=[jax.ShapeDtypeStruct((slots // n_out, width), bf16)] * n_out,
        compiler_params=pltpu.CompilerParams(vmem_limit_bytes=vmem * 1024 * 1024),
        cost_estimate=pl.CostEstimate(
            flops=2 * slots * depth * width,
            bytes_accessed=2 * (slots + depth) * width,
            transcendentals=0,
        ),
    )(select, *pieces, *highs)


def total_kernel(parts, *refs):
    outs = list(refs[3 * len(parts) :])
    for n, part in enumerate(parts):
        own, from_left, from_right = refs[3 * n : 3 * n + 3]
        total = own[...] + from_left[...].astype(f32) + from_right[...].astype(f32)
        wide = total.shape[1] // part
        for m in range(part):
            outs.pop(0)[...] = total[:, m * wide : (m + 1) * wide].astype(bf16)


def totals(owns, arrived, parts):
    in_specs, out_specs, out_shape, args = [], [], [], []
    for own, (from_left, from_right), part in zip(owns, arrived, parts):
        tall, wide = own.shape
        spec = pl.BlockSpec((tall // 4, wide), lambda j: (j, 0))
        in_specs += [spec] * 3
        out_specs += [pl.BlockSpec((tall // 4, wide // part), lambda j: (j, 0))] * part
        out_shape += [jax.ShapeDtypeStruct((tall, wide // part), bf16)] * part
        args += [own, from_left, from_right]
    return pl.pallas_call(
        lambda *refs: total_kernel(parts, *refs),
        grid=(4,),
        in_specs=in_specs,
        out_specs=out_specs,
        out_shape=out_shape,
        compiler_params=pltpu.CompilerParams(vmem_limit_bytes=24 * 1024 * 1024),
        cost_estimate=pl.CostEstimate(
            flops=2 * sum(own.size for own in owns),
            bytes_accessed=10 * sum(own.size for own in owns),
            transcendentals=0,
        ),
    )(*args)


def halves(v):
    middle = v.shape[0] // 2
    return v[:middle], v[middle:]


def per_device(tokens, out_grad, routes, levels, w_gate, w_up, w_down):
    tok, width = tokens.shape
    top = routes.shape[1]
    n_x, n_z, n_y, n_c = [lax.axis_size(axis) for axis in ("x", "z", "y", "c")]
    me_x, me_z, me_y, me_c = [lax.axis_index(axis) for axis in ("x", "z", "y", "c")]
    n_w = n_y * n_c
    n_expert = n_z * n_w
    quarter = width // n_x
    half = width // 2
    ff = w_gate.shape[2]
    group = n_z * CAP
    slots = n_w * group
    block = -(-n_y * CAP // 8) * 8
    sent = n_z * n_c * block
    hop = sent // n_w

    full_pair = lax.all_gather(jnp.concatenate([w_gate[0], w_up[0]], axis=1), "x", axis=0, tiled=True)
    full_down = lax.all_gather(w_down[0], "x", axis=1, tiled=True)

    named = [(routes[:, k : k + 1] == jnp.arange(n_expert)[None, :]).astype(f32) for k in range(top)]
    lower = (jnp.arange(tok)[:, None] > jnp.arange(tok)[None, :]).astype(bf16)
    before = dot(lower, sum(named).astype(bf16))
    rank = [jnp.sum(before * m, axis=1).astype(jnp.int32) for m in named]
    info = jnp.stack(
        [routes[:, k] * CAP + rank[k] for k in range(top)] + [jnp.zeros((tok,), jnp.int32)] * (8 - top), axis=0
    )
    info = lax.all_to_all(
        jnp.broadcast_to(info[None], (n_z,) + info.shape), "z", split_axis=0, concat_axis=0, tiled=True
    )
    t_low, t_high = ring_z(tokens[:, :half], True), ring_z(tokens[:, half:], False, info)

    marks = jnp.concatenate([routes, jnp.stack(rank, axis=1), levels], axis=1).astype(bf16)
    marks = jnp.pad(marks, ((0, 0), (0, 128 - 3 * top)))
    own_g = jnp.concatenate([out_grad, marks], axis=1)
    right_g, left_g = shift(own_g, "y", -1), shift(own_g, "y", 1)
    far_g = shift(halves(right_g)[0], "y", -1), shift(halves(left_g)[1], "y", 1)
    row_g = [own_g, right_g, *far_g, left_g]
    sent_ids = jnp.arange(sent, dtype=jnp.int32)[:, None]
    slot_ids = jnp.arange(slots, dtype=jnp.int32)

    marks = jnp.concatenate([piece[:, width : width + 3 * top] for piece in row_g], axis=0).astype(jnp.int32).T
    expert, rank, level = marks[:top], marks[top : 2 * top], marks[2 * top :]
    source_y = (me_y + jnp.arange(n_y * tok, dtype=jnp.int32) // tok) % n_y
    place = expert // n_w * n_c + expert % n_c
    place = jnp.where(expert // n_c % n_y == me_y, place * block + source_y * CAP + rank, -1)
    gain = level.astype(f32) / 256.0
    pick_gain = sum(jnp.where(sent_ids == place[k : k + 1], gain[k : k + 1], 0.0) for k in range(top)).astype(bf16)

    local = info[:, :top] - me_z * (n_w * CAP)
    here = (local >= 0) & (local < n_w * CAP)
    target, nth = local // CAP, local % CAP
    source_z = jnp.arange(n_z, dtype=jnp.int32)[:, None, None]
    turn = lambda a: lax.dynamic_slice(jnp.concatenate([a, a], axis=0), (me_z, 0, 0), a.shape)
    flat = lambda a, k: a[:, k].reshape(1, n_z * tok)
    away = (target // n_c - me_y + n_y) % n_y * n_c + (target % n_c + me_c) % n_c
    place = turn(jnp.where(here, away * hop + source_z * CAP + nth, -1))
    pick = sum(jnp.where(sent_ids == flat(place, k), 1.0, 0.0) for k in range(top)).astype(bf16)
    home = jnp.where(here, target * group + source_z * CAP + nth, -1)
    spread = sum(jnp.where(flat(home, k).reshape(-1, 1) == slot_ids[None, :], 1.0, 0.0) for k in range(top)).astype(bf16)

    came = jnp.arange(sent, dtype=jnp.int32)[None, :]
    from_y = (me_y - came // hop // n_c + n_y) % n_y
    from_c = (came // hop + me_c) % n_c
    meet = (from_y * n_c + from_c) * group + came % hop
    meet = ((slot_ids[:, None] == meet) & (came % hop < group)).astype(bf16)
    source_w, source_z, nth = slot_ids // group, slot_ids % group // CAP, slot_ids % CAP
    order = (source_z * n_c + source_w % n_c) * block + source_w // n_c * CAP + nth
    order = (order[:, None] == came).astype(bf16)

    (zgrad_sent,) = choose(pick_gain, row_g)
    zgrad_sent = after(zgrad_sent, t_low[n_z // 2], t_high[n_z // 2])
    zgrad = lax.all_to_all(
        zgrad_sent.reshape(n_z * n_c, block, width), ("z", "c"), split_axis=0, concat_axis=0, tiled=True
    ).reshape(sent, width)
    rows = list(choose(pick, t_low, t_high, n_w, 56))
    for n in range(1, n_w):
        dy, dc = n // n_c, n % n_c
        route = [(y * n_c + c, (y + dy) % n_y * n_c + (c + dc) % n_c) for y in range(n_y) for c in range(n_c)]
        rows[n] = lax.ppermute(rows[n], ("y", "c"), route)
    (rows,) = choose(meet, rows, vmem=8)

    def exchange(v):
        v = v.reshape(n_w, group, -1)
        return lax.all_to_all(v, ("y", "c"), split_axis=0, concat_axis=0, tiled=True).reshape(slots, -1)

    pre = dot(rows, full_pair)
    (zgrad,) = choose(order, [after(zgrad, pre)], vmem=8)
    pre_gate, pre_up = pre[:, :ff], pre[:, ff:]
    sigma = jax.nn.sigmoid(pre_gate)
    swish = pre_gate * sigma
    hidden = (swish * pre_up).astype(bf16)
    grad_hidden = dot(zgrad, full_down, COLS1)
    grad_gate = (grad_hidden * pre_up * sigma * (1.0 + pre_gate * (1.0 - sigma))).astype(bf16)
    grad_up = (grad_hidden * swish).astype(bf16)
    grad_pair = jnp.concatenate([grad_gate, grad_up], axis=1)

    back = dot(grad_pair, full_pair, COLS1).astype(bf16)
    back = exchange(back)

    def cols_of(v, q):
        return lax.dynamic_slice(v, (0, (me_x + q) % n_x * quarter), (slots, quarter))

    pair_term = lambda q: dot(cols_of(rows, q), grad_pair, ROWS0)
    down_term = lambda q: dot(hidden, cols_of(zgrad, q), ROWS0)

    def send_far(term):
        far_a, far_b = halves(term(2).astype(bf16))
        return shift(far_a, "x", 1), shift(far_b, "x", -1)

    def toward(term, via_right, via_left):
        right, left = term(1), term(3)
        middle = right.shape[0] // 2
        right = jnp.concatenate([right[:middle] + via_right.astype(f32), right[middle:]], axis=0)
        left = jnp.concatenate([left[:middle], left[middle:] + via_left.astype(f32)], axis=0)
        return right.astype(bf16), left.astype(bf16)

    def send_near(right, left):
        return shift(right, "x", 1), shift(left, "x", -1)

    pair_far, down_far = send_far(pair_term), send_far(down_term)
    pair_near = toward(pair_term, *pair_far)
    down_terms = down_term(1), down_term(3)
    back = after(back, pair_near, down_far, down_terms)
    pair_in = send_near(*pair_near)
    down_in = send_near(*toward(lambda q: down_terms[q // 2], *down_far))

    (column,) = choose(spread, [back], vmem=56)
    grad_tokens = lax.psum_scatter(column, "z", scatter_dimension=0, tiled=True)
    out_gate, out_up, out_down = totals((pair_term(0), down_term(0)), (pair_in, down_in), (2, 1))
    return grad_tokens, out_gate[None], out_up[None], out_down[None]


def solution(mesh):
    n_dp, n_expert = mesh.devices.shape
    inner = 8
    fine = Mesh(mesh.devices.reshape(n_dp, n_expert // inner, inner // 2, 2), ("x", "z", "y", "c"))
    tok = P(("x", "z", "y", "c"), None)
    by_rows = P(("z", "y", "c"), "x", None)
    by_cols = P(("z", "y", "c"), None, "x")
    return jax.shard_map(
        per_device,
        mesh=fine,
        in_specs=(tok, tok, tok, tok, by_rows, by_rows, by_cols),
        out_specs=(tok, by_rows, by_rows, by_cols),
        check_vma=False,
    )
```
